32 devices in a mesh: ctx: 8 (over z, x), tp: 4 (over y, core).
Axes of the slice: x: 2, y: 2, z: 4, core: 2. Of those that a mesh axis runs over, the one named last changes fastest.
Arguments:
- query_in: bfloat16 [4096, 4096], P('ctx', 'tp'), may hold values from -6 to 6
- key_in: bfloat16 [4096, 4096], P('ctx', 'tp'), may hold values from -6 to 6
- value_in: bfloat16 [4096, 4096], P('ctx', 'tp'), may hold values from -6 to 6
- out_grad: bfloat16 [4096, 4096], P('ctx', 'tp'), may hold values from -6 to 6
- doc_ids: int32 [4096], replicated, may hold values from 0 to 3, never falling along the last dimension, each value on 1 to 2048 neighbouring positions
- skip_gain: float32 [4096], P('tp'), may hold values from -4 to 4
- filter_taps: bfloat16 [2048, 8], P(('ctx', 'tp')), may hold values from -0.125 to 0.125
Outputs:
- mixed_out: bfloat16 [4096, 4096], P('ctx', 'tp')
- query_grad: bfloat16 [4096, 4096], P('ctx', 'tp')
- key_grad: bfloat16 [4096, 4096], P('ctx', 'tp')
- value_grad: bfloat16 [4096, 4096], P('ctx', 'tp')
- filter_grad: float32 [2048, 8], P(('ctx', 'tp'))
The draws below stay inside these ranges and needn't reach their ends.
Inputs may be any that keep to these rules, and one draw needn't show every extreme that they name: `doc_ids`: ids never fall along the tokens; each document is 1 to 2048 tokens long and one is exactly 2048 long.
All inputs are finite; a program needn't handle non-finite values.
Results may differ from the reference program's by a relative error of at most 0.0049.
Values may be sent and summed in bfloat16 or wider, within the bound.
A program may use at most 128 MiB of HBM per device.

```python
import math
import jax
import jax.numpy as jnp
import numpy as np
from jax import lax

D = 4096
C = 256
MAXCH = 8
FGROUP = 512
FLEN = 2048
GROUPS = 8
TOKENS = 4096


def block_levels(stream_key, shape, split, low, largest):
    def one(position, blocks):
        steps = jax.random.uniform(jax.random.fold_in(jax.random.fold_in(stream_key, 6), position), (blocks,), jnp.float32, low / len(split), largest / len(split))
        return jnp.repeat(jnp.exp(steps), shape[position] // blocks).reshape((-1,) + (1,) * (len(shape) - position - 1))

    factor_of = one(*split[0])
    for cut in split[1:]:
        factor_of = factor_of * one(*cut)
    return factor_of


def length_profile(amount, total, most, skew):
    weights = [(1 << 20) // math.isqrt(rank ** skew) + 1 for rank in range(2, amount + 1)]
    surplus, counts = total - most - (amount - 1), [1] * (amount - 1)
    while surplus > 0:
        movable = [i for i in range(amount - 1) if counts[i] < most]
        mass, left = sum([weights[i] for i in movable]), surplus
        for i in movable:
            extra = min(most - counts[i], max(1, left * weights[i] // mass), surplus)
            counts[i] = counts[i] + extra
            surplus = surplus - extra
    return np.array([most] + counts)


def uneven(rng, count, total, limit, skew):
    if count == 2:
        one = jax.random.randint(rng, (), max(1, total - limit), min(limit, total - 1) + 1)
        return jnp.stack([one, total - one])
    tallies = jnp.asarray(length_profile(count, total, limit, skew), jnp.int32)
    pairs = (count - 1) // 2
    source_of, receiver = tallies[1:1 + 2 * pairs:2], tallies[2:2 + 2 * pairs:2]
    room = jnp.minimum(source_of - 1, limit - receiver)
    moved = jax.random.randint(jax.random.fold_in(rng, 1), (pairs,), 0, 1 << 20) % (room + 1)
    tallies = tallies.at[1:1 + 2 * pairs:2].set(source_of - moved).at[2:2 + 2 * pairs:2].set(receiver + moved)
    return tallies[jax.random.permutation(jax.random.fold_in(rng, 2), count)]


def gaussian(own_key, extent, deviation, most, pieces=(), held_as=jnp.bfloat16):
    level = block_levels(own_key, extent, pieces, -0.22, 0.18) if pieces else 1.0
    drawn = jax.random.normal(own_key, extent, jnp.float32) * deviation * level
    return jnp.minimum(jnp.maximum(drawn, -most), most).astype(held_as)


def setup_inputs(seed: int = 0) -> dict:
    key_list = jax.random.split(jax.random.key(seed), 8)
    query_in = gaussian(key_list[0], (TOKENS, D), 1.0, 6.0, ((0, 8), (1, 4)))
    key_in = gaussian(key_list[1], (TOKENS, D), 1.0, 6.0, ((0, 8), (1, 4)))
    value_in = gaussian(key_list[2], (TOKENS, D), 1.0, 6.0, ((0, 8), (1, 4)))
    out_grad = gaussian(key_list[3], (TOKENS, D), 1.0, 6.0, ((0, 8), (1, 4)))
    doc_ids = jnp.searchsorted(jnp.cumsum(uneven(key_list[4], 2 * TOKENS // FLEN, TOKENS, FLEN, 2)), jnp.arange(TOKENS), side="right").astype(jnp.int32)
    skip_gain = gaussian(key_list[5], (D,), 1.0, 4.0, ((0, 4),), jnp.float32)
    filter_taps = gaussian(key_list[6], (FLEN, GROUPS), FLEN ** -0.5, 0.125, ((0, 32),))
    return dict(query_in=query_in, key_in=key_in, value_in=value_in, out_grad=out_grad, doc_ids=doc_ids, skip_gain=skip_gain, filter_taps=filter_taps)


def shear_toeplitz(window, stretch):
    groups_n = window.shape[0]
    reverse = window[:, ::-1]
    repeated = jnp.tile(reverse, (1, stretch))
    repeated = repeated[:, :stretch * (2 * stretch - 1)].reshape(groups_n, stretch, 2 * stretch - 1)
    return repeated[:, :, stretch - 1:]

def diagonal_sums(matrix, stretch):
    groups_n = matrix.shape[0]
    flipped = matrix[:, :, ::-1]
    padded = jnp.concatenate([flipped, jnp.zeros_like(flipped)], axis=2)
    flat = padded.reshape(groups_n, 2 * stretch * stretch)[:, :stretch * (2 * stretch - 1)]
    return lax.optimization_barrier(jnp.sum(flat.reshape(groups_n, stretch, 2 * stretch - 1), axis=1))

def pair_mask(ids_reader, ids_source, base):
    stretch = ids_reader.shape[0]
    offset = base + jnp.arange(stretch, dtype=jnp.int32)[:, None] - jnp.arange(stretch, dtype=jnp.int32)[None, :]
    same = ids_reader[:, None] == ids_source[None, :]
    return jnp.where(same & (offset >= 0), 1.0, 0.0).astype(jnp.float32)

def reference(query_in, key_in, value_in, out_grad, doc_ids, skip_gain, filter_taps):
    stretches = TOKENS // C
    mixed_in = (key_in.astype(jnp.float32) * value_in.astype(jnp.float32)).astype(jnp.bfloat16)
    conv_grad = (out_grad.astype(jnp.float32) * query_in.astype(jnp.float32)).astype(jnp.bfloat16)
    sources = mixed_in.reshape(stretches, C, GROUPS, FGROUP)
    grads = conv_grad.reshape(stretches, C, GROUPS, FGROUP)
    segs = doc_ids.reshape(stretches, C)
    taps = filter_taps.T
    blank = jnp.zeros((GROUPS, C), taps.dtype)
    padded = jnp.concatenate([blank, taps, blank], axis=1)
    skip_four = skip_gain.reshape(GROUPS, FGROUP)
    state = skip_four * sources.astype(jnp.float32)
    behind = skip_four * grads.astype(jnp.float32)
    filter_ext = jnp.zeros((GROUPS, (MAXCH + 2) * C), jnp.float32)
    for lag in range(MAXCH + 1):
        tile = shear_toeplitz(padded[:, lag * C:lag * C + 2 * C], C).astype(jnp.float32)
        count = stretches - lag

        def one_pair(items, tile=tile, lag=lag):
            ids_reader, ids_source, source, grad = items
            mask = pair_mask(ids_reader, ids_source, lag * C)
            masked = tile * mask[None]
            source_f = source.astype(jnp.float32)
            grad_f = grad.astype(jnp.float32)
            ahead = jnp.einsum('gab,bgc->agc', masked, source_f, precision=lax.Precision.HIGHEST)
            back_term = jnp.einsum('gab,agc->bgc', masked, grad_f, precision=lax.Precision.HIGHEST)
            product = jnp.einsum('agc,bgc->gab', grad_f, source_f, precision=lax.Precision.HIGHEST) * mask[None]
            return (ahead, back_term, diagonal_sums(product, C))
        ahead, back_term, diags = lax.map(one_pair, (segs[lag:], segs[:count], sources[:count], grads[lag:]))
        state = state.at[lag:].add(ahead)
        behind = behind.at[:count].add(back_term)
        filter_ext = filter_ext.at[:, lag * C:lag * C + 2 * C - 1].add(lax.optimization_barrier(jnp.sum(diags, axis=0)))
    conv = state.reshape(TOKENS, D)
    mixed_out = (query_in.astype(jnp.float32) * conv).astype(jnp.bfloat16)
    query_grad = (out_grad.astype(jnp.float32) * conv).astype(jnp.bfloat16)
    mixed_grad = behind.reshape(TOKENS, D)
    key_grad = (mixed_grad * value_in.astype(jnp.float32)).astype(jnp.bfloat16)
    value_grad = (mixed_grad * key_in.astype(jnp.float32)).astype(jnp.bfloat16)
    scale = 1.0 / math.sqrt(FGROUP * TOKENS)
    filter_grad = (filter_ext[:, C - 1:C - 1 + FLEN] * scale).T
    return (mixed_out, query_grad, key_grad, value_grad, filter_grad)
```

```python
import functools
import math

import jax
import jax.numpy as jnp
from jax import lax
from jax.experimental import pallas as pl
from jax.experimental.pallas import tpu as pltpu
from jax.sharding import PartitionSpec as P

FGROUP = 512
FLEN = 2048
C = 256
BAND = FLEN + C


def band_rows(first):
    wide = jnp.broadcast_to(first, (C, BAND))
    return pltpu.roll(wide, 0, 1, stride=1, stride_axis=0)


def left_diagonals(product):
    total = product[0:8]
    for q in range(1, C // 8):
        total = total + pltpu.roll(product[8 * q : 8 * q + 8], BAND - 8 * q, 1)
    row = lax.broadcasted_iota(jnp.int32, (8, BAND), 0)
    for bit in (1, 2, 4):
        total = jnp.where((row & bit) != 0, pltpu.roll(total, BAND - bit, 1), total)
    return jnp.sum(total, axis=0, keepdims=True)


def conv_kernel(taps_fwd, taps_back, ids_col, ids_src, ids_grd, src, grd, conv, back, diag, acc, wide_f, wide_b):
    rows = conv.shape[0]
    wide_f[...] = band_rows(taps_fwd[...])
    wide_b[...] = band_rows(taps_back[...])
    acc[...] = jnp.zeros_like(acc)

    def stretch(i, carry):
        at = pl.multiple_of(i * C, C)
        ids = ids_col[pl.ds(at, C), :]
        span = pl.ds(at, BAND)
        mask = ids == ids_src[:, span]
        source = src[span, :]
        grad = grd[span, :]
        w = jnp.where(mask, wide_f[...], 0.0).astype(jnp.bfloat16)
        conv[pl.ds(at, C), :] = jnp.dot(w, source, preferred_element_type=jnp.float32).astype(conv.dtype)
        own = grd[pl.ds(at, C), :]
        prod = lax.dot_general(own, source, (((1,), (1,)), ((), ())), preferred_element_type=jnp.float32)
        acc[...] += jnp.where(mask, prod, 0.0)
        w = jnp.where(ids == ids_grd[:, span], wide_b[...], 0.0).astype(jnp.bfloat16)
        back[pl.ds(at, C), :] = jnp.dot(w, grad, preferred_element_type=jnp.float32).astype(back.dtype)
        return carry

    lax.fori_loop(0, rows // C, stretch, 0)
    diag[...] = left_diagonals(acc[...])


def shift_pairs(value, steps):
    count = lax.axis_size("ctx")
    pairs = [(s, s + 2 * steps) for s in range(count) if 0 <= s + 2 * steps < count]
    return lax.ppermute(value, "ctx", pairs)


def shards(query_in, key_in, value_in, out_grad, doc_ids, skip_gain, filter_taps):
    rows, width = query_in.shape
    half = width // 2
    count = lax.axis_size("ctx")
    tps = lax.axis_size("tp")
    here = lax.axis_index("ctx")
    x = here % 2
    pair = here // 2
    big = 2 * rows
    own_taps = filter_taps.shape[0]
    swap = [(s, s ^ 1) for s in range(count)]

    groups = filter_taps.shape[1]
    shared = 2 * tps // groups
    grouped = jnp.repeat(filter_taps.T, shared, axis=0).reshape(1, tps, 2, own_taps).transpose(0, 2, 1, 3)
    grouped = jnp.broadcast_to(grouped, (count // 2, 2, tps, own_taps))
    taps = lax.all_to_all(grouped.reshape(count * tps, own_taps), ("ctx", "tp"), 0, 0, tiled=True)
    taps = taps.reshape(1, FLEN).astype(jnp.float32)
    taps_back = jnp.concatenate([taps, jnp.zeros((1, C), jnp.float32)], axis=1)
    taps_fwd = jnp.concatenate([jnp.zeros((1, 1), jnp.float32), taps[:, ::-1], jnp.zeros((1, C - 1), jnp.float32)], axis=1)

    mixed = (key_in.astype(jnp.float32) * value_in.astype(jnp.float32)).astype(jnp.bfloat16)
    cgrad = (out_grad.astype(jnp.float32) * query_in.astype(jnp.float32)).astype(jnp.bfloat16)
    low = x == 0

    def halves(a):
        keep = jnp.where(low, a[:, :half], a[:, half:])
        give = jnp.where(low, a[:, half:], a[:, :half])
        return keep, give

    def join(keep, got):
        return jnp.where(low, jnp.concatenate([keep, got]), jnp.concatenate([got, keep]))

    mk, mg = halves(mixed)
    gk, gg = halves(cgrad)
    m0 = join(mk, lax.ppermute(mg, "ctx", swap))
    g0 = join(gk, lax.ppermute(gg, "ctx", swap))
    m1 = shift_pairs(m0, 1)
    g1 = shift_pairs(g0, -1)
    m2 = shift_pairs(m1, 1)
    g2 = shift_pairs(g1, -1)
    src = jnp.concatenate([m2, m1, m0])
    grd = jnp.concatenate([g0, g1, g2])

    none = jnp.full((2 * big,), -1, jnp.int32)
    ids = jnp.concatenate([none, doc_ids, none])
    near = lax.dynamic_slice_in_dim(ids, pair * big, 5 * big)
    ids_src = near[: 3 * big].reshape(1, -1)
    ids_grd = near[2 * big :].reshape(1, -1)
    ids_col = near[2 * big : 3 * big].reshape(-1, 1)

    conv, back, diag = pl.pallas_call(
        conv_kernel,
        out_shape=(
            jax.ShapeDtypeStruct((big, half), jnp.bfloat16),
            jax.ShapeDtypeStruct((big, half), jnp.bfloat16),
            jax.ShapeDtypeStruct((1, BAND), jnp.float32),
        ),
        scratch_shapes=[pltpu.VMEM((C, BAND), jnp.float32)] * 3,
        compiler_params=pltpu.CompilerParams(vmem_limit_bytes=56 * 1024 * 1024),
    )(taps_fwd, taps_back, ids_col, ids_src, ids_grd, src, grd)

    lag_sums = diag[:, 1 : FLEN + 1][:, ::-1].reshape(count * tps, own_taps)
    pieces = lax.all_to_all(lag_sums, ("ctx", "tp"), 0, 0, tiled=True)
    scale = 1.0 / math.sqrt(FGROUP * count * rows)
    summed = pieces.reshape(count // 2, 2, tps, own_taps).sum(0) * scale
    filter_grad = summed.transpose(2, 1, 0).reshape(own_taps, groups, shared).sum(2)

    def restore(a):
        keep = jnp.where(low, a[:rows], a[rows:])
        give = jnp.where(low, a[rows:], a[:rows])
        got = lax.ppermute(give, "ctx", swap)
        return jnp.where(low, jnp.concatenate([keep, got], axis=1), jnp.concatenate([got, keep], axis=1)).astype(jnp.float32)

    f32 = lambda a: a.astype(jnp.float32)
    skip = skip_gain[None, :]
    conv = skip * f32(mixed) + restore(conv)
    mgrad = skip * f32(cgrad) + restore(back)
    return (
        (f32(query_in) * conv).astype(jnp.bfloat16),
        (f32(out_grad) * conv).astype(jnp.bfloat16),
        (mgrad * f32(value_in)).astype(jnp.bfloat16),
        (mgrad * f32(key_in)).astype(jnp.bfloat16),
        filter_grad,
    )


def solution(mesh):
    in_specs = (
        P("ctx", "tp"),
        P("ctx", "tp"),
        P("ctx", "tp"),
        P("ctx", "tp"),
        P(),
        P("tp"),
        P(("ctx", "tp"), None),
    )
    out_specs = (
        P("ctx", "tp"),
        P("ctx", "tp"),
        P("ctx", "tp"),
        P("ctx", "tp"),
        P(("ctx", "tp"), None),
    )
    return jax.shard_map(shards, mesh=mesh, in_specs=in_specs, out_specs=out_specs, check_vma=False)
```

```python
import functools
import math

import jax
import jax.numpy as jnp
from jax import lax
from jax.experimental import pallas as pl
from jax.experimental.pallas import tpu as pltpu
from jax.sharding import PartitionSpec as P

FGROUP = 512
FLEN = 2048
C = 256
BAND = FLEN + C
CHUNKS = 2
MESH = pl.DeviceIdType.MESH


def left_diagonals(product):
    total = product[0:8]
    for q in range(1, C // 8):
        total = total + pltpu.roll(product[8 * q : 8 * q + 8], BAND - 8 * q, 1)
    row = lax.broadcasted_iota(jnp.int32, (8, BAND), 0)
    for bit in (1, 2, 4):
        total = jnp.where((row & bit) != 0, pltpu.roll(total, BAND - bit, 1), total)
    return jnp.sum(total, axis=0, keepdims=True)


def pair_kernel(
    half, taps, ids_col, ids_src, ids_grd, query, key, value, ograd,
    conv_out, back_out, diag_out,
    src, grd, give_m, give_g, conv_s, back_s, got_c, got_b,
    taps_all, row_f, row_b, wide, wf, wb, acc, diag_send,
    t_send, t_recv, x_send, x_recv, z_send, z_recv, o_send, o_recv, d_send, d_recv,
):
    count = lax.axis_size("ctx")
    me = lax.axis_index("ctx")
    x = lax.rem(me, 2)
    p = me // 2
    last = count // 2 - 1
    partner = me + 1 - 2 * x
    up = lax.rem(me + 2, count)
    down = lax.rem(me + count - 2, count)
    rows = query.shape[0]
    big = 2 * rows
    chunks, _, cw = src.shape
    tw = taps.shape[1]
    f32 = jnp.float32

    barrier = pltpu.get_barrier_semaphore()
    for d in range(1, count):
        pl.semaphore_signal(barrier, inc=1, device_id={"ctx": lax.rem(me + d, count)}, device_id_type=MESH)
    pl.semaphore_wait(barrier, count - 1)

    def remote(source, target, send, recv, device):
        return pltpu.make_async_remote_copy(
            src_ref=source, dst_ref=target, send_sem=send, recv_sem=recv, device_id={"ctx": device}, device_id_type=MESH
        )

    def at(base, mine):
        offset = x * rows if mine else (1 - x) * rows
        return pl.ds(pl.multiple_of(base + offset, C), rows)

    def columns(own, c):
        offset = x * half if own else (1 - x) * half
        return pl.ds(pl.multiple_of(offset + c * cw, 128), cw)

    tap_copies = [
        remote(taps, taps_all.at[d], t_send.at[d - 1], t_recv.at[d - 1], lax.rem(me + d, count)) for d in range(1, count)
    ]

    def swap_copies(c):
        here = at(0, True)
        return (
            remote(give_m.at[c], src.at[c, at(2 * big, True)], x_send.at[c, 0], x_recv.at[c, 0], partner),
            remote(give_g.at[c], grd.at[c, here], x_send.at[c, 1], x_recv.at[c, 1], partner),
        )

    def hop(c, part, stage):
        mine = part == 0
        index = (c * 2 + part) * 2 + stage
        rising = remote(
            src.at[c, at((2 - stage) * big, mine)], src.at[c, at((1 - stage) * big, mine)],
            z_send.at[0, index], z_recv.at[0, index], up,
        )
        falling = remote(
            grd.at[c, at(stage * big, mine)], grd.at[c, at((1 + stage) * big, mine)],
            z_send.at[1, index], z_recv.at[1, index], down,
        )
        return rising, falling

    def can_send(stage):
        return (p < last) & (p >= stage), (p > 0) & (p <= last - stage)

    def can_receive(stage):
        return p >= 1 + stage, p <= last - 1 - stage

    def start_hop(c, part, stage):
        for copy, ok in zip(hop(c, part, stage), can_send(stage)):
            pl.when(ok)(copy.start)

    def end_hop(c, part, stage):
        for copy, ok in zip(hop(c, part, stage), can_receive(stage)):
            pl.when(ok)(copy.wait_recv)

    for copy in tap_copies:
        copy.start()
    for c in range(chunks):
        cols = columns(False, c)
        give_m[c] = (key[:, cols].astype(f32) * value[:, cols].astype(f32)).astype(jnp.bfloat16)
        swap_copies(c)[0].start()
        give_g[c] = (ograd[:, cols].astype(f32) * query[:, cols].astype(f32)).astype(jnp.bfloat16)
        swap_copies(c)[1].start()
        cols = columns(True, c)
        src[c, at(2 * big, True), :] = (key[:, cols].astype(f32) * value[:, cols].astype(f32)).astype(jnp.bfloat16)
        grd[c, at(0, True), :] = (ograd[:, cols].astype(f32) * query[:, cols].astype(f32)).astype(jnp.bfloat16)
        start_hop(c, 0, 0)

    for stage in range(2):
        low, high = can_receive(stage)

        def blank_src(stage=stage):
            for c in range(chunks):
                src[c, (1 - stage) * big : (2 - stage) * big, :] = jnp.zeros((big, cw), jnp.bfloat16)

        def blank_grd(stage=stage):
            for c in range(chunks):
                grd[c, (1 + stage) * big : (2 + stage) * big, :] = jnp.zeros((big, cw), jnp.bfloat16)

        pl.when(jnp.logical_not(low))(blank_src)
        pl.when(jnp.logical_not(high))(blank_grd)

    taps_all[0] = taps[...]
    for copy in tap_copies:
        copy.wait_recv()
    row_f[...] = jnp.zeros_like(row_f)
    row_b[...] = jnp.zeros_like(row_b)
    own_group = (x * half) // FGROUP
    for j in range(count):
        block = taps_all[lax.rem(me + count - j, count)]
        row_b[:, j * tw : (j + 1) * tw] = jnp.where(own_group == 0, block[0:1], block[1:2])
        m = count - 1 - j
        row_f[:, m * tw : (m + 1) * tw] = jnp.where(own_group == 0, block[2:3], block[3:4])

    def masked(first, shift, ids_row, out):
        wide[...] = pltpu.roll(jnp.broadcast_to(first[...], (C, BAND)), shift, 1, stride=1, stride_axis=0)

        def one(i, carry):
            row = pl.multiple_of(i * C, C)
            mask = ids_col[pl.ds(row, C), :] == ids_row[:, pl.ds(row, BAND)]
            out[i] = jnp.where(mask, wide[...], 0.0).astype(jnp.bfloat16)
            return carry

        lax.fori_loop(0, big // C, one, 0)

    masked(row_f, 1, ids_src, wf)
    end_hop(0, 0, 0)
    start_hop(0, 0, 1)
    masked(row_b, 0, ids_grd, wb)
    acc[...] = jnp.zeros_like(acc)

    def swapped(c):
        for copy in swap_copies(c):
            copy.wait_recv()
        start_hop(c, 1, 0)

    def compute(c):
        def one(i, carry):
            row = pl.multiple_of(i * C, C)
            own, span = pl.ds(row, C), pl.ds(row, BAND)
            source = src[c, span, :]
            conv_s[c, own, :] = jnp.dot(wf[i], source, preferred_element_type=f32).astype(jnp.bfloat16)
            prod = lax.dot_general(grd[c, own, :], source, (((1,), (1,)), ((), ())), preferred_element_type=f32)
            acc[...] += jnp.where(ids_col[own, :] == ids_src[:, span], prod, 0.0)
            back_s[c, own, :] = jnp.dot(wb[i], grd[c, span, :], preferred_element_type=f32).astype(jnp.bfloat16)
            return carry

        lax.fori_loop(0, big // C, one, 0)

    def out_copies(c):
        theirs = at(0, False)
        return (
            remote(conv_s.at[c, theirs], got_c.at[c], o_send.at[c, 0], o_recv.at[c, 0], partner),
            remote(back_s.at[c, theirs], got_b.at[c], o_send.at[c, 1], o_recv.at[c, 1], partner),
        )

    def finish(c):
        cols = columns(True, c)
        conv_out[:, cols] = conv_s[c, at(0, True), :]
        back_out[:, cols] = back_s[c, at(0, True), :]
        for copy in out_copies(c):
            copy.wait_recv()
        cols = columns(False, c)
        conv_out[:, cols] = got_c[c]
        back_out[:, cols] = got_b[c]

    swapped(0)
    end_hop(0, 1, 0)
    start_hop(0, 1, 1)
    for c in range(chunks):
        if c + 1 < chunks:
            end_hop(c + 1, 0, 0)
            start_hop(c + 1, 0, 1)
            swapped(c + 1)
        end_hop(c, 0, 1)
        end_hop(c, 1, 1)
        compute(c)
        for copy in out_copies(c):
            copy.start()
        if c + 1 < chunks:
            end_hop(c + 1, 1, 0)
            start_hop(c + 1, 1, 1)

    sums = pltpu.roll(left_diagonals(acc[...]), BAND - 1, 1)
    wide[0:1, :] = sums
    for j in range(count):
        m = count - 1 - j
        diag_send[j] = jnp.broadcast_to(wide[0:1, m * tw : (m + 1) * tw], (8, tw))
    diag_copies = []
    for d in range(1, count):
        peer = lax.rem(me + d, count)
        diag_copies.append(remote(diag_send.at[peer], diag_out.at[d], d_send.at[d - 1], d_recv.at[d - 1], peer))
    for copy in diag_copies:
        copy.start()
    diag_out[0] = diag_send[me]
    for c in range(chunks):
        finish(c)
    for copy in diag_copies:
        copy.wait_recv()
    for copy in tap_copies + diag_copies:
        copy.wait_send()
    for c in range(chunks):
        for copy in swap_copies(c) + out_copies(c):
            copy.wait_send()
        for part in range(2):
            for stage in range(2):
                for copy, ok in zip(hop(c, part, stage), can_send(stage)):
                    pl.when(ok)(copy.wait_send)


def shards(query_in, key_in, value_in, out_grad, doc_ids, skip_gain, filter_taps):
    rows, width = query_in.shape
    half = width // 2
    chunks = CHUNKS
    cw = half // chunks
    count = lax.axis_size("ctx")
    here = lax.axis_index("ctx")
    pair = here // 2
    big = 2 * rows
    bf16, f32 = jnp.bfloat16, jnp.float32

    local = lax.all_to_all(filter_taps, "tp", split_axis=1, concat_axis=0, tiled=True).T.astype(f32)
    held, tw = local.shape
    both = jnp.broadcast_to(local[:, None], (held, 2 // held, tw)).reshape(2, tw)
    taps = jnp.concatenate([both, both[:, ::-1], jnp.zeros((4, tw), f32)], axis=0)

    none = jnp.full((2 * big,), -1, jnp.int32)
    ids = jnp.concatenate([none, doc_ids, none])
    near = lax.dynamic_slice_in_dim(ids, pair * big, 5 * big)
    ids_src = near[: 3 * big].reshape(1, -1)
    ids_grd = near[2 * big :].reshape(1, -1)
    ids_col = near[2 * big : 3 * big].reshape(-1, 1)

    dma = pltpu.SemaphoreType.DMA
    conv, back, diag = pl.pallas_call(
        functools.partial(pair_kernel, half),
        out_shape=(
            jax.ShapeDtypeStruct((rows, width), bf16),
            jax.ShapeDtypeStruct((rows, width), bf16),
            jax.ShapeDtypeStruct((count, 8, tw), f32),
        ),
        in_specs=[pl.BlockSpec(memory_space=pltpu.VMEM)] * 8,
        out_specs=(pl.BlockSpec(memory_space=pltpu.VMEM),) * 3,
        scratch_shapes=[
            pltpu.VMEM((chunks, 3 * big, cw), bf16),
            pltpu.VMEM((chunks, 3 * big, cw), bf16),
            pltpu.VMEM((chunks, rows, cw), bf16),
            pltpu.VMEM((chunks, rows, cw), bf16),
            pltpu.VMEM((chunks, big, cw), bf16),
            pltpu.VMEM((chunks, big, cw), bf16),
            pltpu.VMEM((chunks, rows, cw), bf16),
            pltpu.VMEM((chunks, rows, cw), bf16),
            pltpu.VMEM((count, 8, tw), f32),
            pltpu.VMEM((1, BAND), f32),
            pltpu.VMEM((1, BAND), f32),
            pltpu.VMEM((C, BAND), f32),
            pltpu.VMEM((big // C, C, BAND), bf16),
            pltpu.VMEM((big // C, C, BAND), bf16),
            pltpu.VMEM((C, BAND), f32),
            pltpu.VMEM((count, 8, tw), f32),
            dma((count - 1,)), dma((count - 1,)),
            dma((chunks, 2)), dma((chunks, 2)),
            dma((2, 4 * chunks)), dma((2, 4 * chunks)),
            dma((chunks, 2)), dma((chunks, 2)),
            dma((count - 1,)), dma((count - 1,)),
        ],
        compiler_params=pltpu.CompilerParams(
            collective_id=0, has_side_effects=True, vmem_limit_bytes=58 * 1024 * 1024
        ),
    )(taps, ids_col, ids_src, ids_grd, query_in, key_in, value_in, out_grad)

    sender = lax.rem(here + count - jnp.arange(count), count)
    odd = (sender % 2 == 1)[:, None]
    each = diag[:, 0, ::-1]
    scale = 1.0 / math.sqrt(FGROUP * count * rows)
    parts = jnp.stack([jnp.where(odd, 0.0, each).sum(0), jnp.where(odd, each, 0.0).sum(0)])
    scaled = parts.reshape(held, 2 // held, tw).sum(1).T * scale
    filter_grad = lax.all_to_all(scaled, "tp", split_axis=0, concat_axis=1, tiled=True)

    skip = skip_gain[None, :]
    key_f, value_f = key_in.astype(f32), value_in.astype(f32)
    query_f, grad_f = query_in.astype(f32), out_grad.astype(f32)
    conv = skip * (key_f * value_f).astype(bf16).astype(f32) + conv.astype(f32)
    mgrad = skip * (grad_f * query_f).astype(bf16).astype(f32) + back.astype(f32)
    return (
        (query_f * conv).astype(bf16),
        (grad_f * conv).astype(bf16),
        (mgrad * value_f).astype(bf16),
        (mgrad * key_f).astype(bf16),
        filter_grad,
    )


def solution(mesh):
    in_specs = (
        P("ctx", "tp"),
        P("ctx", "tp"),
        P("ctx", "tp"),
        P("ctx", "tp"),
        P(),
        P("tp"),
        P(("ctx", "tp"), None),
    )
    out_specs = (
        P("ctx", "tp"),
        P("ctx", "tp"),
        P("ctx", "tp"),
        P("ctx", "tp"),
        P(("ctx", "tp"), None),
    )
    return jax.shard_map(shards, mesh=mesh, in_specs=in_specs, out_specs=out_specs, check_vma=False)
```

```python
import functools
import math

import jax
import jax.numpy as jnp
from jax import lax
from jax.experimental import pallas as pl
from jax.experimental.pallas import tpu as pltpu
from jax.sharding import PartitionSpec as P

FGROUP = 512
FLEN = 2048
C = 256
BAND = FLEN + C
CHUNKS = 4
MESH = pl.DeviceIdType.MESH


def left_diagonals(product):
    total = product[0:8]
    for q in range(1, C // 8):
        total = total + pltpu.roll(product[8 * q : 8 * q + 8], BAND - 8 * q, 1)
    row = lax.broadcasted_iota(jnp.int32, (8, BAND), 0)
    for bit in (1, 2, 4):
        total = jnp.where((row & bit) != 0, pltpu.roll(total, BAND - bit, 1), total)
    return jnp.sum(total, axis=0, keepdims=True)


def pair_kernel(
    half, taps, ids_col, ids_src, ids_grd, query, key, value, ograd,
    conv_out, back_out, diag_out,
    src, grd, give_m, give_g, conv_s, back_s, got_c, got_b,
    taps_all, row_f, row_b, wide, wf, wb, acc, diag_send,
    t_send, t_recv, x_send, x_recv, z_send, z_recv, o_send, o_recv, d_send, d_recv,
):
    count = lax.axis_size("ctx")
    me = lax.axis_index("ctx")
    x = lax.rem(me, 2)
    p = me // 2
    last = count // 2 - 1
    partner = me + 1 - 2 * x
    up = lax.rem(me + 2, count)
    down = lax.rem(me + count - 2, count)
    rows = query.shape[0]
    big = 2 * rows
    chunks, _, cw = src.shape
    tw = taps.shape[1]
    f32 = jnp.float32

    barrier = pltpu.get_barrier_semaphore()
    for d in range(1, count):
        pl.semaphore_signal(barrier, inc=1, device_id={"ctx": lax.rem(me + d, count)}, device_id_type=MESH)
    pl.semaphore_wait(barrier, count - 1)

    def remote(source, target, send, recv, device):
        return pltpu.make_async_remote_copy(
            src_ref=source, dst_ref=target, send_sem=send, recv_sem=recv, device_id={"ctx": device}, device_id_type=MESH
        )

    def at(base, mine):
        offset = x * rows if mine else (1 - x) * rows
        return pl.ds(pl.multiple_of(base + offset, C), rows)

    def columns(own, c):
        offset = x * half if own else (1 - x) * half
        return pl.ds(pl.multiple_of(offset + c * cw, 128), cw)

    tap_copies = [
        remote(taps, taps_all.at[d], t_send.at[d - 1], t_recv.at[d - 1], lax.rem(me + d, count)) for d in range(1, count)
    ]

    def swap_copies(c):
        here = at(0, True)
        return (
            remote(give_m.at[c], src.at[c, at(2 * big, True)], x_send.at[c, 0], x_recv.at[c, 0], partner),
            remote(give_g.at[c], grd.at[c, here], x_send.at[c, 1], x_recv.at[c, 1], partner),
        )

    def hop(c, part, stage):
        mine = part == 0
        index = (c * 2 + part) * 2 + stage
        rising = remote(
            src.at[c, at((2 - stage) * big, mine)], src.at[c, at((1 - stage) * big, mine)],
            z_send.at[0, index], z_recv.at[0, index], up,
        )
        falling = remote(
            grd.at[c, at(stage * big, mine)], grd.at[c, at((1 + stage) * big, mine)],
            z_send.at[1, index], z_recv.at[1, index], down,
        )
        return rising, falling

    def can_send(stage):
        return (p < last) & (p >= stage), (p > 0) & (p <= last - stage)

    def can_receive(stage):
        return p >= 1 + stage, p <= last - 1 - stage

    def start_hop(c, part, stage):
        for copy, ok in zip(hop(c, part, stage), can_send(stage)):
            pl.when(ok)(copy.start)

    def end_hop(c, part, stage):
        for copy, ok in zip(hop(c, part, stage), can_receive(stage)):
            pl.when(ok)(copy.wait_recv)

    for copy in tap_copies:
        copy.start()
    def begin(c):
        if c >= chunks:
            return
        cols = columns(False, c)
        give_m[c] = (key[:, cols].astype(f32) * value[:, cols].astype(f32)).astype(jnp.bfloat16)
        swap_copies(c)[0].start()
        give_g[c] = (ograd[:, cols].astype(f32) * query[:, cols].astype(f32)).astype(jnp.bfloat16)
        swap_copies(c)[1].start()
        cols = columns(True, c)
        src[c, at(2 * big, True), :] = (key[:, cols].astype(f32) * value[:, cols].astype(f32)).astype(jnp.bfloat16)
        grd[c, at(0, True), :] = (ograd[:, cols].astype(f32) * query[:, cols].astype(f32)).astype(jnp.bfloat16)
        start_hop(c, 0, 0)

    begin(0)
    begin(1)

    for stage in range(2):
        low, high = can_receive(stage)

        def blank_src(stage=stage):
            for c in range(chunks):
                src[c, (1 - stage) * big : (2 - stage) * big, :] = jnp.zeros((big, cw), jnp.bfloat16)

        def blank_grd(stage=stage):
            for c in range(chunks):
                grd[c, (1 + stage) * big : (2 + stage) * big, :] = jnp.zeros((big, cw), jnp.bfloat16)

        pl.when(jnp.logical_not(low))(blank_src)
        pl.when(jnp.logical_not(high))(blank_grd)

    taps_all[0] = taps[...]
    for copy in tap_copies:
        copy.wait_recv()
    row_f[...] = jnp.zeros_like(row_f)
    row_b[...] = jnp.zeros_like(row_b)
    own_group = (x * half) // FGROUP
    for j in range(count):
        block = taps_all[lax.rem(me + count - j, count)]
        row_b[:, j * tw : (j + 1) * tw] = jnp.where(own_group == 0, block[0:1], block[1:2])
        m = count - 1 - j
        row_f[:, m * tw : (m + 1) * tw] = jnp.where(own_group == 0, block[2:3], block[3:4])

    def masked(first, shift, ids_row, out):
        wide[...] = pltpu.roll(jnp.broadcast_to(first[...], (C, BAND)), shift, 1, stride=1, stride_axis=0)

        def one(i, carry):
            row = pl.multiple_of(i * C, C)
            mask = ids_col[pl.ds(row, C), :] == ids_row[:, pl.ds(row, BAND)]
            out[i] = jnp.where(mask, wide[...], 0.0).astype(jnp.bfloat16)
            return carry

        lax.fori_loop(0, big // C, one, 0)

    masked(row_f, 1, ids_src, wf)
    end_hop(0, 0, 0)
    start_hop(0, 0, 1)
    masked(row_b, 0, ids_grd, wb)
    acc[...] = jnp.zeros_like(acc)

    def swapped(c):
        for copy in swap_copies(c):
            copy.wait_recv()
        start_hop(c, 1, 0)
        begin(c + 2)

    def compute(c, first, end):
        def one(i, carry):
            row = pl.multiple_of(i * C, C)
            own, span = pl.ds(row, C), pl.ds(row, BAND)
            source = src[c, span, :]
            conv_s[c, own, :] = jnp.dot(wf[i], source, preferred_element_type=f32).astype(jnp.bfloat16)
            prod = lax.dot_general(grd[c, own, :], source, (((1,), (1,)), ((), ())), preferred_element_type=f32)
            acc[...] += jnp.where(ids_col[own, :] == ids_src[:, span], prod, 0.0)
            back_s[c, own, :] = jnp.dot(wb[i], grd[c, span, :], preferred_element_type=f32).astype(jnp.bfloat16)
            return carry

        lax.fori_loop(first, end, one, 0)

    def out_copies(c):
        theirs = at(0, False)
        return (
            remote(conv_s.at[c, theirs], got_c.at[c], o_send.at[c, 0], o_recv.at[c, 0], partner),
            remote(back_s.at[c, theirs], got_b.at[c], o_send.at[c, 1], o_recv.at[c, 1], partner),
        )

    def finish(c):
        cols = columns(True, c)
        conv_out[:, cols] = conv_s[c, at(0, True), :]
        back_out[:, cols] = back_s[c, at(0, True), :]
        for copy in out_copies(c):
            copy.wait_recv()
        cols = columns(False, c)
        conv_out[:, cols] = got_c[c]
        back_out[:, cols] = got_b[c]

    def forward_first(c):
        if c < chunks:
            end_hop(c, 0, 0)
            start_hop(c, 0, 1)
            swapped(c)

    def forward_second(c):
        if c < chunks:
            end_hop(c, 1, 0)
            start_hop(c, 1, 1)

    swapped(0)
    forward_second(0)
    forward_first(1)
    middle = big // C // 2
    for c in range(chunks):
        forward_first(c + 2)
        end_hop(c, 0, 1)
        end_hop(c, 1, 1)
        compute(c, 0, middle)
        forward_second(c + 1)
        compute(c, middle, big // C)
        for copy in out_copies(c):
            copy.start()

    sums = pltpu.roll(left_diagonals(acc[...]), BAND - 1, 1)
    wide[0:1, :] = sums
    for j in range(count):
        m = count - 1 - j
        diag_send[j] = jnp.broadcast_to(wide[0:1, m * tw : (m + 1) * tw], (8, tw))
    diag_copies = []
    for d in range(1, count):
        peer = lax.rem(me + d, count)
        diag_copies.append(remote(diag_send.at[peer], diag_out.at[d], d_send.at[d - 1], d_recv.at[d - 1], peer))
    for copy in diag_copies:
        copy.start()
    diag_out[0] = diag_send[me]
    for c in range(chunks):
        finish(c)
    for copy in diag_copies:
        copy.wait_recv()
    for copy in tap_copies + diag_copies:
        copy.wait_send()
    for c in range(chunks):
        for copy in swap_copies(c) + out_copies(c):
            copy.wait_send()
        for part in range(2):
            for stage in range(2):
                for copy, ok in zip(hop(c, part, stage), can_send(stage)):
                    pl.when(ok)(copy.wait_send)


def shards(query_in, key_in, value_in, out_grad, doc_ids, skip_gain, filter_taps):
    rows, width = query_in.shape
    half = width // 2
    chunks = max(1, min(CHUNKS, half // 128))
    cw = half // chunks
    count = lax.axis_size("ctx")
    here = lax.axis_index("ctx")
    pair = here // 2
    big = 2 * rows
    bf16, f32 = jnp.bfloat16, jnp.float32

    local = lax.all_to_all(filter_taps, "tp", split_axis=1, concat_axis=0, tiled=True).T.astype(f32)
    held, tw = local.shape
    both = jnp.broadcast_to(local[:, None], (held, 2 // held, tw)).reshape(2, tw)
    taps = jnp.concatenate([both, both[:, ::-1], jnp.zeros((4, tw), f32)], axis=0)

    none = jnp.full((2 * big,), -1, jnp.int32)
    ids = jnp.concatenate([none, doc_ids, none])
    near = lax.dynamic_slice_in_dim(ids, pair * big, 5 * big)
    ids_src = near[: 3 * big].reshape(1, -1)
    ids_grd = near[2 * big :].reshape(1, -1)
    ids_col = near[2 * big : 3 * big].reshape(-1, 1)

    dma = pltpu.SemaphoreType.DMA
    conv, back, diag = pl.pallas_call(
        functools.partial(pair_kernel, half),
        out_shape=(
            jax.ShapeDtypeStruct((rows, width), bf16),
            jax.ShapeDtypeStruct((rows, width), bf16),
            jax.ShapeDtypeStruct((count, 8, tw), f32),
        ),
        in_specs=[pl.BlockSpec(memory_space=pltpu.VMEM)] * 8,
        out_specs=(pl.BlockSpec(memory_space=pltpu.VMEM),) * 3,
        scratch_shapes=[
            pltpu.VMEM((chunks, 3 * big, cw), bf16),
            pltpu.VMEM((chunks, 3 * big, cw), bf16),
            pltpu.VMEM((chunks, rows, cw), bf16),
            pltpu.VMEM((chunks, rows, cw), bf16),
            pltpu.VMEM((chunks, big, cw), bf16),
            pltpu.VMEM((chunks, big, cw), bf16),
            pltpu.VMEM((chunks, rows, cw), bf16),
            pltpu.VMEM((chunks, rows, cw), bf16),
            pltpu.VMEM((count, 8, tw), f32),
            pltpu.VMEM((1, BAND), f32),
            pltpu.VMEM((1, BAND), f32),
            pltpu.VMEM((C, BAND), f32),
            pltpu.VMEM((big // C, C, BAND), bf16),
            pltpu.VMEM((big // C, C, BAND), bf16),
            pltpu.VMEM((C, BAND), f32),
            pltpu.VMEM((count, 8, tw), f32),
            dma((count - 1,)), dma((count - 1,)),
            dma((chunks, 2)), dma((chunks, 2)),
            dma((2, 4 * chunks)), dma((2, 4 * chunks)),
            dma((chunks, 2)), dma((chunks, 2)),
            dma((count - 1,)), dma((count - 1,)),
        ],
        compiler_params=pltpu.CompilerParams(
            collective_id=0, has_side_effects=True, vmem_limit_bytes=58 * 1024 * 1024
        ),
    )(taps, ids_col, ids_src, ids_grd, query_in, key_in, value_in, out_grad)

    sender = lax.rem(here + count - jnp.arange(count), count)
    odd = (sender % 2 == 1)[:, None]
    each = diag[:, 0, ::-1]
    scale = 1.0 / math.sqrt(FGROUP * count * rows)
    parts = jnp.stack([jnp.where(odd, 0.0, each).sum(0), jnp.where(odd, each, 0.0).sum(0)])
    scaled = parts.reshape(held, 2 // held, tw).sum(1).T * scale
    filter_grad = lax.all_to_all(scaled, "tp", split_axis=0, concat_axis=1, tiled=True)

    skip = skip_gain[None, :]
    key_f, value_f = key_in.astype(f32), value_in.astype(f32)
    query_f, grad_f = query_in.astype(f32), out_grad.astype(f32)
    conv = skip * lax.reduce_precision(key_f * value_f, 8, 7) + conv.astype(f32)
    mgrad = skip * lax.reduce_precision(grad_f * query_f, 8, 7) + back.astype(f32)
    return (
        (query_f * conv).astype(bf16),
        (grad_f * conv).astype(bf16),
        (mgrad * value_f).astype(bf16),
        (mgrad * key_f).astype(bf16),
        filter_grad,
    )


def solution(mesh):
    in_specs = (
        P("ctx", "tp"),
        P("ctx", "tp"),
        P("ctx", "tp"),
        P("ctx", "tp"),
        P(),
        P("tp"),
        P(("ctx", "tp"), None),
    )
    out_specs = (
        P("ctx", "tp"),
        P("ctx", "tp"),
        P("ctx", "tp"),
        P("ctx", "tp"),
        P(("ctx", "tp"), None),
    )
    return jax.shard_map(shards, mesh=mesh, in_specs=in_specs, out_specs=out_specs, check_vma=False)
```

```python
import functools
import math

import jax
import jax.numpy as jnp
from jax import lax
from jax.experimental import pallas as pl
from jax.experimental.pallas import tpu as pltpu
from jax.sharding import PartitionSpec as P

FGROUP = 512
FLEN = 2048
C = 256
BAND = FLEN + C
CHUNKS = 4
MESH = pl.DeviceIdType.MESH


def left_diagonals(product):
    total = product[0:8]
    for q in range(1, C // 8):
        total = total + pltpu.roll(product[8 * q : 8 * q + 8], BAND - 8 * q, 1)
    row = lax.broadcasted_iota(jnp.int32, (8, BAND), 0)
    for bit in (1, 2, 4):
        total = jnp.where((row & bit) != 0, pltpu.roll(total, BAND - bit, 1), total)
    return jnp.sum(total, axis=0, keepdims=True)


def pair_kernel(
    half, taps_tp, ids_col, ids_src, ids_grd, query, key, value, ograd,
    conv_out, back_out, sums_out,
    src, grd, give_m, give_g, conv_s, back_s, got_c, got_b,
    taps_all, row_f, row_b, wide, wf, wb, acc, diag_send, diag_in, taps, taps_in, sums_send, sums_in,
    t_send, t_recv, x_send, x_recv, z_send, z_recv, o_send, o_recv, d_send, d_recv, a_send, a_recv, b_send, b_recv,
):
    count = lax.axis_size("ctx")
    me = lax.axis_index("ctx")
    x = lax.rem(me, 2)
    p = me // 2
    last = count // 2 - 1
    partner = me + 1 - 2 * x
    up = lax.rem(me + 2, count)
    down = lax.rem(me + count - 2, count)
    rows = query.shape[0]
    big = 2 * rows
    chunks, _, cw = src.shape
    tw = taps.shape[1]
    f32 = jnp.float32

    barrier = pltpu.get_barrier_semaphore()
    for d in range(1, count):
        pl.semaphore_signal(barrier, inc=1, device_id={"ctx": lax.rem(me + d, count)}, device_id_type=MESH)
    tps = lax.axis_size("tp")
    lane = lax.axis_index("tp")
    for d in range(1, tps):
        pl.semaphore_signal(barrier, inc=1, device_id={"tp": lax.rem(lane + d, tps)}, device_id_type=MESH)
    pl.semaphore_wait(barrier, count - 1 + tps - 1)
    own_taps = taps_tp.shape[2]
    held = sums_out.shape[0] // tps

    def remote(source, target, send, recv, device, axis="ctx"):
        return pltpu.make_async_remote_copy(
            src_ref=source, dst_ref=target, send_sem=send, recv_sem=recv, device_id={axis: device}, device_id_type=MESH
        )

    def at(base, mine):
        offset = x * rows if mine else (1 - x) * rows
        return pl.ds(pl.multiple_of(base + offset, C), rows)

    def columns(own, c):
        offset = x * half if own else (1 - x) * half
        return pl.ds(pl.multiple_of(offset + c * cw, 128), cw)

    tap_copies = [
        remote(taps, taps_all.at[d], t_send.at[d - 1], t_recv.at[d - 1], lax.rem(me + d, count)) for d in range(1, count)
    ]

    def swap_copies(c):
        here = at(0, True)
        return (
            remote(give_m.at[c], src.at[c, at(2 * big, True)], x_send.at[c, 0], x_recv.at[c, 0], partner),
            remote(give_g.at[c], grd.at[c, here], x_send.at[c, 1], x_recv.at[c, 1], partner),
        )

    def hop(c, part, stage):
        mine = part == 0
        index = (c * 2 + part) * 2 + stage
        rising = remote(
            src.at[c, at((2 - stage) * big, mine)], src.at[c, at((1 - stage) * big, mine)],
            z_send.at[0, index], z_recv.at[0, index], up,
        )
        falling = remote(
            grd.at[c, at(stage * big, mine)], grd.at[c, at((1 + stage) * big, mine)],
            z_send.at[1, index], z_recv.at[1, index], down,
        )
        return rising, falling

    def can_send(stage):
        return (p < last) & (p >= stage), (p > 0) & (p <= last - stage)

    def can_receive(stage):
        return p >= 1 + stage, p <= last - 1 - stage

    def start_hop(c, part, stage):
        for copy, ok in zip(hop(c, part, stage), can_send(stage)):
            pl.when(ok)(copy.start)

    def end_hop(c, part, stage):
        for copy, ok in zip(hop(c, part, stage), can_receive(stage)):
            pl.when(ok)(copy.wait_recv)

    first_copies = []
    for d in range(1, tps):
        peer = lax.rem(lane + d, tps)
        first_copies.append(remote(taps_tp.at[peer], taps_in.at[d], a_send.at[d - 1], a_recv.at[d - 1], peer, "tp"))
    for copy in first_copies:
        copy.start()
    def begin(c):
        if c >= chunks:
            return
        cols = columns(False, c)
        give_m[c] = (key[:, cols].astype(f32) * value[:, cols].astype(f32)).astype(jnp.bfloat16)
        swap_copies(c)[0].start()
        give_g[c] = (ograd[:, cols].astype(f32) * query[:, cols].astype(f32)).astype(jnp.bfloat16)
        swap_copies(c)[1].start()
        cols = columns(True, c)
        src[c, at(2 * big, True), :] = (key[:, cols].astype(f32) * value[:, cols].astype(f32)).astype(jnp.bfloat16)
        grd[c, at(0, True), :] = (ograd[:, cols].astype(f32) * query[:, cols].astype(f32)).astype(jnp.bfloat16)
        start_hop(c, 0, 0)

    begin(0)
    begin(1)

    for stage in range(2):
        low, high = can_receive(stage)

        def blank_src(stage=stage):
            for c in range(chunks):
                src[c, (1 - stage) * big : (2 - stage) * big, :] = jnp.zeros((big, cw), jnp.bfloat16)

        def blank_grd(stage=stage):
            for c in range(chunks):
                grd[c, (1 + stage) * big : (2 + stage) * big, :] = jnp.zeros((big, cw), jnp.bfloat16)

        pl.when(jnp.logical_not(low))(blank_src)
        pl.when(jnp.logical_not(high))(blank_grd)

    taps_in[0] = taps_tp[lane]
    for copy in first_copies:
        copy.wait_recv()
    for t in range(tps):
        block = taps_in[lax.rem(lane + tps - t, tps)]
        taps[0:2, t * own_taps : (t + 1) * own_taps] = block[0:2]
        m = tps - 1 - t
        taps[2:4, m * own_taps : (m + 1) * own_taps] = block[2:4]
    taps[4:8, :] = jnp.zeros((4, tw), f32)
    for copy in tap_copies:
        copy.start()
    taps_all[0] = taps[...]
    def swapped(c):
        for copy in swap_copies(c):
            copy.wait_recv()
        start_hop(c, 1, 0)
        begin(c + 2)

    def forward_first(c):
        if c < chunks:
            end_hop(c, 0, 0)
            start_hop(c, 0, 1)
            swapped(c)

    def forward_second(c):
        if c < chunks:
            end_hop(c, 1, 0)
            start_hop(c, 1, 1)

    forward_first(0)
    forward_second(0)
    forward_first(1)

    for copy in tap_copies:
        copy.wait_recv()
    row_f[...] = jnp.zeros_like(row_f)
    row_b[...] = jnp.zeros_like(row_b)
    own_group = (x * half) // FGROUP
    for j in range(count):
        block = taps_all[lax.rem(me + count - j, count)]
        row_b[:, j * tw : (j + 1) * tw] = jnp.where(own_group == 0, block[0:1], block[1:2])
        m = count - 1 - j
        row_f[:, m * tw : (m + 1) * tw] = jnp.where(own_group == 0, block[2:3], block[3:4])

    def masked(first, shift, ids_row, out):
        wide[...] = pltpu.roll(jnp.broadcast_to(first[...], (C, BAND)), shift, 1, stride=1, stride_axis=0)

        def one(i, carry):
            row = pl.multiple_of(i * C, C)
            mask = ids_col[pl.ds(row, C), :] == ids_row[:, pl.ds(row, BAND)]
            out[i] = jnp.where(mask, wide[...], 0.0).astype(jnp.bfloat16)
            return carry

        lax.fori_loop(0, big // C, one, 0)

    masked(row_f, 1, ids_src, wf)
    masked(row_b, 0, ids_grd, wb)
    acc[...] = jnp.zeros_like(acc)

    def compute(c, first, end):
        def one(i, carry):
            row = pl.multiple_of(i * C, C)
            own, span = pl.ds(row, C), pl.ds(row, BAND)
            source = src[c, span, :]
            conv_s[c, own, :] = jnp.dot(wf[i], source, preferred_element_type=f32).astype(jnp.bfloat16)
            prod = lax.dot_general(grd[c, own, :], source, (((1,), (1,)), ((), ())), preferred_element_type=f32)
            acc[...] += jnp.where(ids_col[own, :] == ids_src[:, span], prod, 0.0)
            back_s[c, own, :] = jnp.dot(wb[i], grd[c, span, :], preferred_element_type=f32).astype(jnp.bfloat16)
            return carry

        lax.fori_loop(first, end, one, 0)

    def out_copies(c):
        theirs = at(0, False)
        return (
            remote(conv_s.at[c, theirs], got_c.at[c], o_send.at[c, 0], o_recv.at[c, 0], partner),
            remote(back_s.at[c, theirs], got_b.at[c], o_send.at[c, 1], o_recv.at[c, 1], partner),
        )

    def finish(c):
        cols = columns(True, c)
        conv_out[:, cols] = conv_s[c, at(0, True), :]
        back_out[:, cols] = back_s[c, at(0, True), :]
        for copy in out_copies(c):
            copy.wait_recv()
        cols = columns(False, c)
        conv_out[:, cols] = got_c[c]
        back_out[:, cols] = got_b[c]

    middle = big // C // 2
    for c in range(chunks):
        forward_first(c + 2)
        end_hop(c, 0, 1)
        end_hop(c, 1, 1)
        compute(c, 0, middle)
        forward_second(c + 1)
        compute(c, middle, big // C)
        for copy in out_copies(c):
            copy.start()

    sums = pltpu.roll(left_diagonals(acc[...]), BAND - 1, 1)
    wide[0:1, :] = sums
    for j in range(count):
        m = count - 1 - j
        diag_send[j] = jnp.broadcast_to(wide[0:1, m * tw : (m + 1) * tw], (8, tw))
    diag_copies = []
    for d in range(1, count):
        peer = lax.rem(me + d, count)
        diag_copies.append(remote(diag_send.at[peer], diag_in.at[d], d_send.at[d - 1], d_recv.at[d - 1], peer))
    for copy in diag_copies:
        copy.start()
    diag_in[0] = diag_send[me]
    for c in range(chunks - 1):
        finish(c)
    for copy in diag_copies:
        copy.wait_recv()
    even = jnp.zeros((1, tw), f32)
    odd = jnp.zeros((1, tw), f32)
    for d in range(count):
        term = diag_in[d, 0:1]
        flip = lax.rem(me + count - d, 2) == 1
        even = even + jnp.where(flip, 0.0, term)
        odd = odd + jnp.where(flip, term, 0.0)
    if held == 1:
        even = even + odd
    wide[0:1, 0:tw] = even
    wide[1:2, 0:tw] = odd
    for t in range(tps):
        m = tps - 1 - t
        sums_send[t, 0:2, :] = wide[0:2, m * own_taps : (m + 1) * own_taps]
        sums_send[t, 2:8, :] = jnp.zeros((6, own_taps), f32)
    last_copies = []
    for d in range(1, tps):
        peer = lax.rem(lane + d, tps)
        last_copies.append(remote(sums_send.at[peer], sums_in.at[d], b_send.at[d - 1], b_recv.at[d - 1], peer, "tp"))
    for copy in last_copies:
        copy.start()
    sums_in[0] = sums_send[lane]
    finish(chunks - 1)
    for copy in last_copies:
        copy.wait_recv()
    for t in range(tps):
        sums_out[t * held : (t + 1) * held, :] = sums_in[lax.rem(lane + tps - t, tps), 0:held]
    for copy in first_copies + tap_copies + diag_copies + last_copies:
        copy.wait_send()
    for c in range(chunks):
        for copy in swap_copies(c) + out_copies(c):
            copy.wait_send()
        for part in range(2):
            for stage in range(2):
                for copy, ok in zip(hop(c, part, stage), can_send(stage)):
                    pl.when(ok)(copy.wait_send)


def shards(query_in, key_in, value_in, out_grad, doc_ids, skip_gain, filter_taps):
    rows, width = query_in.shape
    half = width // 2
    chunks = max(1, min(CHUNKS, half // 128))
    cw = half // chunks
    count = lax.axis_size("ctx")
    here = lax.axis_index("ctx")
    pair = here // 2
    big = 2 * rows
    bf16, f32 = jnp.bfloat16, jnp.float32

    tps = lax.axis_size("tp")
    own_taps, groups = filter_taps.shape
    held = groups // tps
    tw = own_taps * tps
    grouped = filter_taps.T.astype(f32).reshape(tps, held, 1, own_taps)
    grouped = jnp.broadcast_to(grouped, (tps, held, 2 // held, own_taps)).reshape(tps, 2, own_taps)
    taps_tp = jnp.concatenate([grouped, grouped[:, :, ::-1], jnp.zeros((tps, 4, own_taps), f32)], axis=1)

    none = jnp.full((2 * big,), -1, jnp.int32)
    ids = jnp.concatenate([none, doc_ids, none])
    near = lax.dynamic_slice_in_dim(ids, pair * big, 5 * big)
    ids_src = near[: 3 * big].reshape(1, -1)
    ids_grd = near[2 * big :].reshape(1, -1)
    ids_col = near[2 * big : 3 * big].reshape(-1, 1)

    dma = pltpu.SemaphoreType.DMA
    conv, back, sums = pl.pallas_call(
        functools.partial(pair_kernel, half),
        out_shape=(
            jax.ShapeDtypeStruct((rows, width), bf16),
            jax.ShapeDtypeStruct((rows, width), bf16),
            jax.ShapeDtypeStruct((groups, own_taps), f32),
        ),
        in_specs=[pl.BlockSpec(memory_space=pltpu.VMEM)] * 8,
        out_specs=(pl.BlockSpec(memory_space=pltpu.VMEM),) * 3,
        scratch_shapes=[
            pltpu.VMEM((chunks, 3 * big, cw), bf16),
            pltpu.VMEM((chunks, 3 * big, cw), bf16),
            pltpu.VMEM((chunks, rows, cw), bf16),
            pltpu.VMEM((chunks, rows, cw), bf16),
            pltpu.VMEM((chunks, big, cw), bf16),
            pltpu.VMEM((chunks, big, cw), bf16),
            pltpu.VMEM((chunks, rows, cw), bf16),
            pltpu.VMEM((chunks, rows, cw), bf16),
            pltpu.VMEM((count, 8, tw), f32),
            pltpu.VMEM((1, BAND), f32),
            pltpu.VMEM((1, BAND), f32),
            pltpu.VMEM((C, BAND), f32),
            pltpu.VMEM((big // C, C, BAND), bf16),
            pltpu.VMEM((big // C, C, BAND), bf16),
            pltpu.VMEM((C, BAND), f32),
            pltpu.VMEM((count, 8, tw), f32),
            pltpu.VMEM((count, 8, tw), f32),
            pltpu.VMEM((8, tw), f32),
            pltpu.VMEM((tps, 8, own_taps), f32),
            pltpu.VMEM((tps, 8, own_taps), f32),
            pltpu.VMEM((tps, 8, own_taps), f32),
            dma((count - 1,)), dma((count - 1,)),
            dma((chunks, 2)), dma((chunks, 2)),
            dma((2, 4 * chunks)), dma((2, 4 * chunks)),
            dma((chunks, 2)), dma((chunks, 2)),
            dma((count - 1,)), dma((count - 1,)),
            dma((tps - 1,)), dma((tps - 1,)),
            dma((tps - 1,)), dma((tps - 1,)),
        ],
        compiler_params=pltpu.CompilerParams(
            collective_id=0, has_side_effects=True, vmem_limit_bytes=58 * 1024 * 1024
        ),
    )(taps_tp, ids_col, ids_src, ids_grd, query_in, key_in, value_in, out_grad)

    scale = 1.0 / math.sqrt(FGROUP * count * rows)
    filter_grad = sums[:, ::-1].T * scale

    skip = skip_gain[None, :]
    key_f, value_f = key_in.astype(f32), value_in.astype(f32)
    query_f, grad_f = query_in.astype(f32), out_grad.astype(f32)
    conv = skip * lax.reduce_precision(key_f * value_f, 8, 7) + conv.astype(f32)
    mgrad = skip * lax.reduce_precision(grad_f * query_f, 8, 7) + back.astype(f32)
    return (
        (query_f * conv).astype(bf16),
        (grad_f * conv).astype(bf16),
        (mgrad * value_f).astype(bf16),
        (mgrad * key_f).astype(bf16),
        filter_grad,
    )


def solution(mesh):
    in_specs = (
        P("ctx", "tp"),
        P("ctx", "tp"),
        P("ctx", "tp"),
        P("ctx", "tp"),
        P(),
        P("tp"),
        P(("ctx", "tp"), None),
    )
    out_specs = (
        P("ctx", "tp"),
        P("ctx", "tp"),
        P("ctx", "tp"),
        P("ctx", "tp"),
        P(("ctx", "tp"), None),
    )
    return jax.shard_map(shards, mesh=mesh, in_specs=in_specs, out_specs=out_specs, check_vma=False)
```

```python
import functools
import math

import jax
import jax.numpy as jnp
from jax import lax
from jax.experimental import pallas as pl
from jax.experimental.pallas import tpu as pltpu
from jax.sharding import PartitionSpec as P

FGROUP = 512
FLEN = 2048
C = 256
BAND = FLEN + C
CHUNKS = 4
MESH = pl.DeviceIdType.MESH


def left_diagonals(product):
    total = product[0:8]
    for q in range(1, C // 8):
        total = total + pltpu.roll(product[8 * q : 8 * q + 8], BAND - 8 * q, 1)
    row = lax.broadcasted_iota(jnp.int32, (8, BAND), 0)
    for bit in (1, 2, 4):
        total = jnp.where((row & bit) != 0, pltpu.roll(total, BAND - bit, 1), total)
    return jnp.sum(total, axis=0, keepdims=True)


def pair_kernel(
    half, taps_tp, ids_col, ids_src, ids_grd, query, key, value, ograd,
    conv_out, back_out, sums_out,
    src, grd, give_m, give_g, conv_s, back_s, got_c, got_b,
    taps_all, row_f, row_b, wide, wf, wb, acc, conv_near, back_near, diag_send, diag_in, taps, taps_in, sums_send, sums_in,
    t_send, t_recv, x_send, x_recv, z_send, z_recv, o_send, o_recv, d_send, d_recv, a_send, a_recv, b_send, b_recv,
):
    count = lax.axis_size("ctx")
    me = lax.axis_index("ctx")
    x = lax.rem(me, 2)
    p = me // 2
    last = count // 2 - 1
    partner = me + 1 - 2 * x
    up = lax.rem(me + 2, count)
    down = lax.rem(me + count - 2, count)
    rows = query.shape[0]
    big = 2 * rows
    chunks, _, cw = src.shape
    tw = taps.shape[1]
    f32 = jnp.float32

    barrier = pltpu.get_barrier_semaphore()
    for d in range(1, count):
        pl.semaphore_signal(barrier, inc=1, device_id={"ctx": lax.rem(me + d, count)}, device_id_type=MESH)
    tps = lax.axis_size("tp")
    lane = lax.axis_index("tp")
    for d in range(1, tps):
        pl.semaphore_signal(barrier, inc=1, device_id={"tp": lax.rem(lane + d, tps)}, device_id_type=MESH)
    pl.semaphore_wait(barrier, count - 1 + tps - 1)
    own_taps = taps_tp.shape[2]
    held = sums_out.shape[0] // tps

    def remote(source, target, send, recv, device, axis="ctx"):
        return pltpu.make_async_remote_copy(
            src_ref=source, dst_ref=target, send_sem=send, recv_sem=recv, device_id={axis: device}, device_id_type=MESH
        )

    def at(base, mine):
        offset = x * rows if mine else (1 - x) * rows
        return pl.ds(pl.multiple_of(base + offset, C), rows)

    def columns(own, c):
        offset = x * half if own else (1 - x) * half
        return pl.ds(pl.multiple_of(offset + c * cw, 128), cw)

    tap_copies = [
        remote(taps, taps_all.at[d], t_send.at[d - 1], t_recv.at[d - 1], lax.rem(me + d, count)) for d in range(1, count)
    ]

    def swap_copies(c):
        here = at(0, True)
        return (
            remote(give_m.at[c], src.at[c, at(2 * big, True)], x_send.at[c, 0], x_recv.at[c, 0], partner),
            remote(give_g.at[c], grd.at[c, here], x_send.at[c, 1], x_recv.at[c, 1], partner),
        )

    def hop(c, part, stage):
        mine = part == 0
        index = (c * 2 + part) * 2 + stage
        rising = remote(
            src.at[c, at((2 - stage) * big, mine)], src.at[c, at((1 - stage) * big, mine)],
            z_send.at[0, index], z_recv.at[0, index], up,
        )
        falling = remote(
            grd.at[c, at(stage * big, mine)], grd.at[c, at((1 + stage) * big, mine)],
            z_send.at[1, index], z_recv.at[1, index], down,
        )
        return rising, falling

    def can_send(stage):
        return (p < last) & (p >= stage), (p > 0) & (p <= last - stage)

    def can_receive(stage):
        return p >= 1 + stage, p <= last - 1 - stage

    def start_hop(c, part, stage):
        for copy, ok in zip(hop(c, part, stage), can_send(stage)):
            pl.when(ok)(copy.start)

    def end_hop(c, part, stage):
        for copy, ok in zip(hop(c, part, stage), can_receive(stage)):
            pl.when(ok)(copy.wait_recv)

    first_copies = []
    for d in range(1, tps):
        peer = lax.rem(lane + d, tps)
        first_copies.append(remote(taps_tp.at[peer], taps_in.at[d], a_send.at[d - 1], a_recv.at[d - 1], peer, "tp"))
    for copy in first_copies:
        copy.start()
    def begin(c):
        if c >= chunks:
            return
        cols = columns(False, c)
        give_m[c] = (key[:, cols].astype(f32) * value[:, cols].astype(f32)).astype(jnp.bfloat16)
        swap_copies(c)[0].start()
        give_g[c] = (ograd[:, cols].astype(f32) * query[:, cols].astype(f32)).astype(jnp.bfloat16)
        swap_copies(c)[1].start()
        cols = columns(True, c)
        src[c, at(2 * big, True), :] = (key[:, cols].astype(f32) * value[:, cols].astype(f32)).astype(jnp.bfloat16)
        grd[c, at(0, True), :] = (ograd[:, cols].astype(f32) * query[:, cols].astype(f32)).astype(jnp.bfloat16)
        start_hop(c, 0, 0)

    begin(0)
    begin(1)

    for stage in range(2):
        low, high = can_receive(stage)

        def blank_src(stage=stage):
            for c in range(chunks):
                src[c, (1 - stage) * big : (2 - stage) * big, :] = jnp.zeros((big, cw), jnp.bfloat16)

        def blank_grd(stage=stage):
            for c in range(chunks):
                grd[c, (1 + stage) * big : (2 + stage) * big, :] = jnp.zeros((big, cw), jnp.bfloat16)

        pl.when(jnp.logical_not(low))(blank_src)
        pl.when(jnp.logical_not(high))(blank_grd)

    taps_in[0] = taps_tp[lane]
    for copy in first_copies:
        copy.wait_recv()
    for t in range(tps):
        block = taps_in[lax.rem(lane + tps - t, tps)]
        taps[0:2, t * own_taps : (t + 1) * own_taps] = block[0:2]
        m = tps - 1 - t
        taps[2:4, m * own_taps : (m + 1) * own_taps] = block[2:4]
    taps[4:8, :] = jnp.zeros((4, tw), f32)
    for copy in tap_copies:
        copy.start()
    taps_all[0] = taps[...]
    def swapped(c):
        for copy in swap_copies(c):
            copy.wait_recv()
        start_hop(c, 1, 0)
        begin(c + 2)

    def forward_first(c):
        if c < chunks:
            end_hop(c, 0, 0)
            start_hop(c, 0, 1)
            swapped(c)

    def forward_second(c):
        if c < chunks:
            end_hop(c, 1, 0)
            start_hop(c, 1, 1)

    forward_first(0)
    forward_second(0)
    forward_first(1)

    for copy in tap_copies:
        copy.wait_recv()
    row_f[...] = jnp.zeros_like(row_f)
    row_b[...] = jnp.zeros_like(row_b)
    own_group = (x * half) // FGROUP
    for j in range(count):
        block = taps_all[lax.rem(me + count - j, count)]
        row_b[:, j * tw : (j + 1) * tw] = jnp.where(own_group == 0, block[0:1], block[1:2])
        m = count - 1 - j
        row_f[:, m * tw : (m + 1) * tw] = jnp.where(own_group == 0, block[2:3], block[3:4])

    def masked(first, shift, ids_row, out):
        wide[...] = pltpu.roll(jnp.broadcast_to(first[...], (C, BAND)), shift, 1, stride=1, stride_axis=0)

        def one(i, carry):
            row = pl.multiple_of(i * C, C)
            mask = ids_col[pl.ds(row, C), :] == ids_row[:, pl.ds(row, BAND)]
            out[i] = jnp.where(mask, wide[...], 0.0).astype(jnp.bfloat16)
            return carry

        lax.fori_loop(0, big // C, one, 0)

    masked(row_f, 1, ids_src, wf)
    masked(row_b, 0, ids_grd, wb)
    acc[...] = jnp.zeros_like(acc)

    split = big + C

    def near(c):
        def one(i, carry):
            row = pl.multiple_of(i * C, C)
            own, span = pl.ds(row, C), pl.ds(row + big, BAND - big)
            source = src[c, span, :]
            conv_near[own, :] = jnp.dot(wf[i, :, big:], source, preferred_element_type=f32)
            prod = lax.dot_general(grd[c, own, :], source, (((1,), (1,)), ((), ())), preferred_element_type=f32)
            acc[:, big:] += jnp.where(ids_col[own, :] == ids_src[:, span], prod, 0.0)
            back_near[own, :] = jnp.dot(wb[i, :, :split], grd[c, pl.ds(row, split), :], preferred_element_type=f32)
            return carry

        lax.fori_loop(0, big // C, one, 0)

    def far(c):
        def one(i, carry):
            row = pl.multiple_of(i * C, C)
            own, span = pl.ds(row, C), pl.ds(row, big)
            source = src[c, span, :]
            ahead = jnp.dot(wf[i, :, :big], source, preferred_element_type=f32)
            conv_s[c, own, :] = (conv_near[own, :] + ahead).astype(jnp.bfloat16)
            prod = lax.dot_general(grd[c, own, :], source, (((1,), (1,)), ((), ())), preferred_element_type=f32)
            acc[:, :big] += jnp.where(ids_col[own, :] == ids_src[:, span], prod, 0.0)
            behind = jnp.dot(wb[i, :, split:], grd[c, pl.ds(row + split, BAND - split), :], preferred_element_type=f32)
            back_s[c, own, :] = (back_near[own, :] + behind).astype(jnp.bfloat16)
            return carry

        lax.fori_loop(0, big // C, one, 0)

    def out_copies(c):
        theirs = at(0, False)
        return (
            remote(conv_s.at[c, theirs], got_c.at[c], o_send.at[c, 0], o_recv.at[c, 0], partner),
            remote(back_s.at[c, theirs], got_b.at[c], o_send.at[c, 1], o_recv.at[c, 1], partner),
        )

    def finish(c):
        cols = columns(True, c)
        conv_out[:, cols] = conv_s[c, at(0, True), :]
        back_out[:, cols] = back_s[c, at(0, True), :]
        for copy in out_copies(c):
            copy.wait_recv()
        cols = columns(False, c)
        conv_out[:, cols] = got_c[c]
        back_out[:, cols] = got_b[c]

    for c in range(chunks):
        forward_first(c + 2)
        near(c)
        forward_second(c + 1)
        end_hop(c, 0, 1)
        end_hop(c, 1, 1)
        far(c)
        for copy in out_copies(c):
            copy.start()

    sums = pltpu.roll(left_diagonals(acc[...]), BAND - 1, 1)
    wide[0:1, :] = sums
    for j in range(count):
        m = count - 1 - j
        diag_send[j] = jnp.broadcast_to(wide[0:1, m * tw : (m + 1) * tw], (8, tw))
    diag_copies = []
    for d in range(1, count):
        peer = lax.rem(me + d, count)
        diag_copies.append(remote(diag_send.at[peer], diag_in.at[d], d_send.at[d - 1], d_recv.at[d - 1], peer))
    for copy in diag_copies:
        copy.start()
    diag_in[0] = diag_send[me]
    for c in range(chunks - 1):
        finish(c)
    for copy in diag_copies:
        copy.wait_recv()
    even = jnp.zeros((1, tw), f32)
    odd = jnp.zeros((1, tw), f32)
    for d in range(count):
        term = diag_in[d, 0:1]
        flip = lax.rem(me + count - d, 2) == 1
        even = even + jnp.where(flip, 0.0, term)
        odd = odd + jnp.where(flip, term, 0.0)
    if held == 1:
        even = even + odd
    wide[0:1, 0:tw] = even
    wide[1:2, 0:tw] = odd
    for t in range(tps):
        m = tps - 1 - t
        sums_send[t, 0:2, :] = wide[0:2, m * own_taps : (m + 1) * own_taps]
        sums_send[t, 2:8, :] = jnp.zeros((6, own_taps), f32)
    last_copies = []
    for d in range(1, tps):
        peer = lax.rem(lane + d, tps)
        last_copies.append(remote(sums_send.at[peer], sums_in.at[d], b_send.at[d - 1], b_recv.at[d - 1], peer, "tp"))
    for copy in last_copies:
        copy.start()
    sums_in[0] = sums_send[lane]
    finish(chunks - 1)
    for copy in last_copies:
        copy.wait_recv()
    for t in range(tps):
        sums_out[t * held : (t + 1) * held, :] = sums_in[lax.rem(lane + tps - t, tps), 0:held]
    for copy in first_copies + tap_copies + diag_copies + last_copies:
        copy.wait_send()
    for c in range(chunks):
        for copy in swap_copies(c) + out_copies(c):
            copy.wait_send()
        for part in range(2):
            for stage in range(2):
                for copy, ok in zip(hop(c, part, stage), can_send(stage)):
                    pl.when(ok)(copy.wait_send)


def shards(query_in, key_in, value_in, out_grad, doc_ids, skip_gain, filter_taps):
    rows, width = query_in.shape
    half = width // 2
    chunks = max(1, min(CHUNKS, half // 128))
    cw = half // chunks
    count = lax.axis_size("ctx")
    here = lax.axis_index("ctx")
    pair = here // 2
    big = 2 * rows
    bf16, f32 = jnp.bfloat16, jnp.float32

    tps = lax.axis_size("tp")
    own_taps, groups = filter_taps.shape
    held = groups // tps
    tw = own_taps * tps
    grouped = filter_taps.T.astype(f32).reshape(tps, held, 1, own_taps)
    grouped = jnp.broadcast_to(grouped, (tps, held, 2 // held, own_taps)).reshape(tps, 2, own_taps)
    taps_tp = jnp.concatenate([grouped, grouped[:, :, ::-1], jnp.zeros((tps, 4, own_taps), f32)], axis=1)

    none = jnp.full((2 * big,), -1, jnp.int32)
    ids = jnp.concatenate([none, doc_ids, none])
    near = lax.dynamic_slice_in_dim(ids, pair * big, 5 * big)
    ids_src = near[: 3 * big].reshape(1, -1)
    ids_grd = near[2 * big :].reshape(1, -1)
    ids_col = near[2 * big : 3 * big].reshape(-1, 1)

    dma = pltpu.SemaphoreType.DMA
    conv, back, sums = pl.pallas_call(
        functools.partial(pair_kernel, half),
        out_shape=(
            jax.ShapeDtypeStruct((rows, width), bf16),
            jax.ShapeDtypeStruct((rows, width), bf16),
            jax.ShapeDtypeStruct((groups, own_taps), f32),
        ),
        in_specs=[pl.BlockSpec(memory_space=pltpu.VMEM)] * 8,
        out_specs=(pl.BlockSpec(memory_space=pltpu.VMEM),) * 3,
        scratch_shapes=[
            pltpu.VMEM((chunks, 3 * big, cw), bf16),
            pltpu.VMEM((chunks, 3 * big, cw), bf16),
            pltpu.VMEM((chunks, rows, cw), bf16),
            pltpu.VMEM((chunks, rows, cw), bf16),
            pltpu.VMEM((chunks, big, cw), bf16),
            pltpu.VMEM((chunks, big, cw), bf16),
            pltpu.VMEM((chunks, rows, cw), bf16),
            pltpu.VMEM((chunks, rows, cw), bf16),
            pltpu.VMEM((count, 8, tw), f32),
            pltpu.VMEM((1, BAND), f32),
            pltpu.VMEM((1, BAND), f32),
            pltpu.VMEM((C, BAND), f32),
            pltpu.VMEM((big // C, C, BAND), bf16),
            pltpu.VMEM((big // C, C, BAND), bf16),
            pltpu.VMEM((C, BAND), f32),
            pltpu.VMEM((big, cw), f32),
            pltpu.VMEM((big, cw), f32),
            pltpu.VMEM((count, 8, tw), f32),
            pltpu.VMEM((count, 8, tw), f32),
            pltpu.VMEM((8, tw), f32),
            pltpu.VMEM((tps, 8, own_taps), f32),
            pltpu.VMEM((tps, 8, own_taps), f32),
            pltpu.VMEM((tps, 8, own_taps), f32),
            dma((count - 1,)), dma((count - 1,)),
            dma((chunks, 2)), dma((chunks, 2)),
            dma((2, 4 * chunks)), dma((2, 4 * chunks)),
            dma((chunks, 2)), dma((chunks, 2)),
            dma((count - 1,)), dma((count - 1,)),
            dma((tps - 1,)), dma((tps - 1,)),
            dma((tps - 1,)), dma((tps - 1,)),
        ],
        compiler_params=pltpu.CompilerParams(
            collective_id=0, has_side_effects=True, vmem_limit_bytes=58 * 1024 * 1024
        ),
    )(taps_tp, ids_col, ids_src, ids_grd, query_in, key_in, value_in, out_grad)

    scale = 1.0 / math.sqrt(FGROUP * count * rows)
    filter_grad = sums[:, ::-1].T * scale

    skip = skip_gain[None, :]
    key_f, value_f = key_in.astype(f32), value_in.astype(f32)
    query_f, grad_f = query_in.astype(f32), out_grad.astype(f32)
    conv = skip * lax.reduce_precision(key_f * value_f, 8, 7) + conv.astype(f32)
    mgrad = skip * lax.reduce_precision(grad_f * query_f, 8, 7) + back.astype(f32)
    return (
        (query_f * conv).astype(bf16),
        (grad_f * conv).astype(bf16),
        (mgrad * value_f).astype(bf16),
        (mgrad * key_f).astype(bf16),
        filter_grad,
    )


def solution(mesh):
    in_specs = (
        P("ctx", "tp"),
        P("ctx", "tp"),
        P("ctx", "tp"),
        P("ctx", "tp"),
        P(),
        P("tp"),
        P(("ctx", "tp"), None),
    )
    out_specs = (
        P("ctx", "tp"),
        P("ctx", "tp"),
        P("ctx", "tp"),
        P("ctx", "tp"),
        P(("ctx", "tp"), None),
    )
    return jax.shard_map(shards, mesh=mesh, in_specs=in_specs, out_specs=out_specs, check_vma=False)
```
